32 devices in a mesh: parts: 2 (over y), space: 4 (over z), src: 2 (over x), depth: 2 (over core).
Axes of the slice: x: 2, y: 2, z: 4, core: 2. Of those that a mesh axis runs over, the one named last changes fastest.
Arguments:
- start_fields: float32 [4, 3, 16, 128, 128], P(('parts', 'src'), None, 'space', 'depth'), parts along dimension 0, may hold values from -6 to 6
- adjoint_fields: float32 [4, 3, 16, 128, 128], P(('parts', 'src'), None, 'space', 'depth'), parts along dimension 0, may hold values from -6 to 6
- conductivity: float32 [32, 128, 128], P(('parts', 'space'), 'depth'), parts along dimension 0, may hold values from 0.02 to 0.5
- surface_rows: int32 [32, 128], P(('parts', 'space')), parts along dimension 0, may hold values from 0 to 16
- source_cells: int32 [4], P(('parts', 'src')), parts along dimension 0, may hold values from 0 to 262143
Outputs:
- fields: float32 [4, 3, 16, 128, 128], P(('parts', 'src'), None, 'space', 'depth'), parts along dimension 0
- gradient: float32 [32, 128, 128], P(('parts', 'space'), 'depth', 'src'), parts along dimension 0
The draws below stay inside these ranges and needn't reach their ends.
There are 2 independent parts, one for each index of `parts`. The reference program is written for one: setup_inputs(seed, part) draws one part's arguments, and reference() takes and returns one part's arrays. A program takes and returns all parts, laid end to end along the dimension named above; each array names one. Nothing has to cross between parts.
Inputs may be any that keep to these rules, and one draw needn't show every extreme that they name: `source_cells`: flat cell index (x * 128 + z) * 128 + y. `surface_rows`: rows above it are air.
All inputs are finite; a program needn't handle non-finite values.
Results may differ from the reference program's by a relative error of at most 0.0001.
Values sent between devices are 32-bit elements; how exact they have to be, the bound alone decides.
A program may use at most 64 MiB of HBM per device.

```python
import math
import jax
import jax.numpy as jnp

NY = 128
ITERS = 3
AIR_ROWS = 16
NX = 16
NZ = 128
SOURCES = 2


def with_ends(values, own_key, low, largest):
    index_at = [jax.random.randint(jax.random.fold_in(own_key, axis), (), 0, length) for axis, length in enumerate(values.shape)]
    main_axis = values.shape.index(max(values.shape))
    neighbour = index_at[:main_axis] + [(index_at[main_axis] + 1) % values.shape[main_axis]] + index_at[main_axis + 1:]
    return values.at[tuple(index_at)].set(low).at[tuple(neighbour)].set(largest)


def shard_levels(own_key, shape, cuts, smallest, largest):
    level, own = 1.0, jax.random.fold_in(own_key, 6)
    for position, blocks in cuts:
        heights = jnp.exp(jax.random.uniform(jax.random.fold_in(own, position), (blocks,), jnp.float32, smallest / len(cuts), largest / len(cuts)))
        level = level * jnp.repeat(heights, shape[position] // blocks).reshape([-1 if axis == position else 1 for axis in range(len(shape))])
    return level


def normal_values(own_key, dims, spread, bound, cuts=(), kind=jnp.bfloat16):
    level = shard_levels(own_key, dims, cuts, -0.22, 0.18) if cuts else 1.0
    values = jax.random.normal(own_key, dims, jnp.float32) * spread * level
    return jnp.minimum(jnp.maximum(values, -bound), bound).astype(kind)


def setup_inputs(seed: int = 0, part: int = 0) -> dict:
    key_list = jax.random.split(jax.random.key(seed), 6)
    part_splits = jax.random.split(jax.random.fold_in(key_list[5], part), 6)
    start_fields = normal_values(part_splits[0], (SOURCES, 3, NX, NZ, NY), 1.0, 6.0, ((0, 2), (2, 4), (3, 2)), jnp.float32)
    adjoint_fields = normal_values(part_splits[1], (SOURCES, 3, NX, NZ, NY), 1.0, 6.0, ((0, 2), (2, 4), (3, 2)), jnp.float32)
    conductivity = jnp.clip(jnp.exp(math.log(0.5) - 3.218876 * jax.random.uniform(part_splits[2], (NX, NZ, NY), jnp.float32) ** shard_levels(part_splits[2], (NX, NZ, NY), ((0, 4), (1, 2)), -0.2, 0.2)), 0.02, 0.5)
    surface_rows = with_ends(jax.random.randint(part_splits[3], (NX, NY), 0, AIR_ROWS + 1), jax.random.fold_in(part_splits[3], 1), 0, AIR_ROWS).astype(jnp.int32)
    source_cells = jax.random.randint(part_splits[4], (SOURCES,), 0, NX * NZ * NY).astype(jnp.int32)
    return {"start_fields": start_fields, "adjoint_fields": adjoint_fields, "conductivity": conductivity, "surface_rows": surface_rows, "source_cells": source_cells}


ALPHA = 2.0
AIR = 0.01
SOURCE_AMP = 10.0


def curl_apply(padded, mass):
    e0 = padded[:, 0]
    e1 = padded[:, 1]
    e2 = padded[:, 2]

    def fwd_x(f):
        return f[:, 1:, :-1, :-1] - f[:, :-1, :-1, :-1]

    def fwd_z(f):
        return f[:, :-1, 1:, :-1] - f[:, :-1, :-1, :-1]

    def fwd_y(f):
        return f[:, :-1, :-1, 1:] - f[:, :-1, :-1, :-1]

    def back_x(h):
        return h[:, 1:, 1:, 1:] - h[:, :-1, 1:, 1:]

    def back_z(h):
        return h[:, 1:, 1:, 1:] - h[:, 1:, :-1, 1:]

    def back_y(h):
        return h[:, 1:, 1:, 1:] - h[:, 1:, 1:, :-1]

    curl_x = fwd_y(e2) - fwd_z(e1)
    curl_y = fwd_z(e0) - fwd_x(e2)
    curl_z = fwd_x(e1) - fwd_y(e0)
    out_x = back_y(curl_z) - back_z(curl_y)
    out_y = back_z(curl_x) - back_x(curl_z)
    out_z = back_x(curl_y) - back_y(curl_x)
    inner = padded[:, :, 1:-1, 1:-1, 1:-1]
    return jnp.stack((out_x, out_y, out_z), axis=1) + mass * inner


def column(vals):
    return vals[:, None, None, None, None]


def inner_sum(left, right):
    return jnp.sum(left * right, axis=(1, 2, 3, 4))


def reference(start_fields, adjoint_fields, conductivity, surface_rows, source_cells):
    rows = jnp.arange(NZ, dtype=jnp.int32)
    earth = rows[None, :, None] >= surface_rows[:, None, :]
    sigma = jnp.where(earth, conductivity, AIR)
    mass = ALPHA * sigma
    flat = ((jnp.arange(NX, dtype=jnp.int32)[:, None, None] * NZ + rows[None, :, None]) * NY
            + jnp.arange(NY, dtype=jnp.int32)[None, None, :])
    onehot = jnp.where(flat[None] == source_cells[:, None, None, None], SOURCE_AMP, 0.0).astype(start_fields.dtype)
    blank = jnp.zeros_like(onehot)
    rhs = jnp.stack((onehot, blank, blank), axis=1)

    def apply(field):
        return curl_apply(jnp.pad(field, ((0, 0), (0, 0), (1, 1), (1, 1), (1, 1))), mass)

    x = start_fields
    r = rhs - apply(x)
    r0 = r
    rho = inner_sum(r0, r)
    p = r
    for step in range(ITERS):
        v = apply(p)
        alpha = rho / inner_sum(r0, v)
        s = r - column(alpha) * v
        t = apply(s)
        omega = inner_sum(t, s) / inner_sum(t, t)
        x = x + column(alpha) * p + column(omega) * s
        r = s - column(omega) * t
        if step + 1 < ITERS:
            rho_new = inner_sum(r0, r)
            beta = (rho_new / rho) * (alpha / omega)
            p = r + column(beta) * (p - column(omega) * v)
            rho = rho_new
    total = jnp.sum(x * adjoint_fields, axis=(0, 1))
    gradient = jnp.where(earth, (-ALPHA * sigma) * total, 0.0)
    return x, gradient
```

```python
import functools

import jax
import jax.numpy as jnp
from jax import lax
from jax.experimental import pallas as pl
from jax.experimental.pallas import tpu as pltpu
from jax.sharding import PartitionSpec as P

ITERS = 3
ALPHA = 2.0
AIR = 0.01
SOURCE_AMP = 10.0
CENTRE = 6.5
HALF = 6.5
DEGREE = 2 * ITERS
APPLIES = DEGREE + 1
PAD = 8
MESH = pl.DeviceIdType.MESH


def times_operator(poly):
    out = [None] * (len(poly) + 1)

    def add(k, term):
        out[k] = term if out[k] is None else out[k] + term

    for k, c in enumerate(poly):
        add(k, CENTRE * c)
        if k == 0:
            add(1, HALF * c)
        else:
            add(k + 1, (0.5 * HALF) * c)
            add(k - 1, (0.5 * HALF) * c)
    return out


def axpy(a, scale, b):
    out = []
    for k in range(max(len(a), len(b))):
        if k >= len(b):
            out.append(a[k])
        elif k >= len(a):
            out.append(scale * b[k])
        else:
            out.append(a[k] + scale * b[k])
    return out


def with_first(poly, moments):
    total = poly[0] * moments[0]
    for k in range(1, len(poly)):
        total = total + poly[k] * moments[k]
    return total


def inner(a, b, moments):
    total = None
    for i, u in enumerate(a):
        row = None
        for j, w in enumerate(b):
            term = w * (0.5 * (moments[i + j] + moments[abs(i - j)]))
            row = term if row is None else row + term
        total = u * row if total is None else total + u * row
    return total


def field_coefficients(moments):
    one = jnp.ones_like(moments[0])
    r = [one]
    p = [one]
    rho = moments[0]
    x = []
    for step in range(ITERS):
        v = times_operator(p)
        alpha = rho / with_first(v, moments)
        s = axpy(r, -alpha, v)
        t = times_operator(s)
        omega = inner(t, s, moments) / inner(t, t, moments)
        x = axpy(axpy(x, alpha, p), omega, s)
        if step + 1 < ITERS:
            r = axpy(s, -omega, t)
            rho_new = with_first(r, moments)
            beta = rho_new / rho * (alpha / omega)
            p = axpy(r, beta, axpy(p, -omega, v))
            rho = rho_new
    return x


def kernel(
    sizes,
    start_ref,
    adj_ref,
    cond_ref,
    surf_ref,
    cell_ref,
    out_ref,
    grad_ref,
    basis,
    right_in,
    left_in,
    left_out,
    rows_out,
    rows_in,
    mass,
    dots,
    dots_out,
    dots_in,
    share_out,
    share_in,
    load_sem,
    send_sem,
    recv_sem,
    dot_send,
    dot_recv,
    share_send,
    share_recv,
):
    n_space, n_src, cx, cz, cy = sizes
    group = n_space * 2
    share = cy // n_src
    last = cx - 1
    s = lax.axis_index("space")
    d = lax.axis_index("depth")
    c = lax.axis_index("src")
    me = s * 2 + d

    def member(k):
        g = lax.rem(me + k, group)
        return {"space": g // 2, "depth": lax.rem(g, 2)}

    def source(k):
        return {"src": lax.rem(c + k, n_src)}

    barrier = pltpu.get_barrier_semaphore()

    def greet(k, carry):
        pl.semaphore_signal(barrier, inc=1, device_id=member(k), device_id_type=MESH)
        return carry

    lax.fori_loop(1, group, greet, 0)
    for k in range(1, n_src):
        pl.semaphore_signal(barrier, inc=1, device_id=source(k), device_id_type=MESH)

    own = pl.ds(PAD, cz)
    load = pltpu.make_async_copy(start_ref.at[0], basis.at[0, :, :, own, :], load_sem)
    load.start()

    lane = lax.broadcasted_iota(jnp.int32, (cz, cy), 1)
    row = lax.broadcasted_iota(jnp.int32, (cz, cy), 0)
    first_lane = lane == 0
    last_lane = lane == cy - 1
    z_start = d * cz
    zero_row = jnp.zeros((1, cy), jnp.float32)

    def earth(x):
        return (z_start + row) >= surf_ref[pl.ds(x, 1), :]

    for x in range(cx):
        mass[x] = ALPHA * jnp.where(earth(x), cond_ref[x], AIR)
    zero_rows = jnp.zeros((3, cx, 1, cy), jnp.float32)

    def clear(j, carry):
        basis[j, :, :, PAD - 1 : PAD, :] = zero_rows
        basis[j, :, :, PAD + cz : PAD + cz + 1, :] = zero_rows
        right_in[j, 1, PAD - 1 : PAD, :] = zero_row
        rows_out[j] = jnp.zeros((16, cy), jnp.float32)
        return carry

    lax.fori_loop(0, APPLIES, clear, 0)

    @pl.when(s == 0)
    def _():
        left_in[...] = jnp.zeros(left_in.shape, jnp.float32)

    @pl.when(s == n_space - 1)
    def _():
        def blank(j, carry):
            right_in[j, :, own, :] = jnp.zeros((2, cz, cy), jnp.float32)
            return carry

        lax.fori_loop(0, APPLIES, blank, 0)

    def before(f):
        return jnp.where(first_lane, 0.0, pltpu.roll(f, 1, 1))

    def after(f):
        return jnp.where(last_lane, 0.0, pltpu.roll(f, cy - 1, 1))

    def copy(j, kind):
        if kind == 0:
            src, dst, where = left_out.at[j], left_in.at[j], {"space": s + 1}
        elif kind == 1:
            src = basis.at[j, pl.ds(1, 2), 0, own, :]
            dst, where = right_in.at[j, :, own, :], {"space": s - 1}
        else:
            src, dst = rows_out.at[j], rows_in.at[j, kind - 2]
            where = {"depth": 1 - d}
            if kind == 3:
                where["space"] = s + 1
            elif kind == 4:
                where["space"] = s - 1
        return pltpu.make_async_remote_copy(
            src_ref=src,
            dst_ref=dst,
            send_sem=send_sem.at[j, kind],
            recv_sem=recv_sem.at[j, kind],
            device_id=where,
            device_id_type=MESH,
        )

    has_left = s > 0
    has_right = s < n_space - 1

    def send_right(j):
        e0 = basis[j, 0, last, own, :]
        left_out[j, 0] = basis[j, 1, last, own, :] + after(e0) - e0
        left_out[j, 1] = basis[j, 2, last, own, :] + basis[j, 0, last, pl.ds(PAD + 1, cz), :] - e0

        @pl.when(has_right)
        def _():
            copy(j, 0).start()

    def send_left(j):
        @pl.when(has_left)
        def _():
            copy(j, 1).start()

    edge = PAD + (cz - 1) * (1 - d)

    def send_rows(j):
        for q in range(3):
            for x in range(cx):
                rows_out[j, q * cx + x : q * cx + x + 1, :] = basis[j, q, x, pl.ds(edge, 1), :]
        copy(j, 2).start()

        @pl.when(has_right)
        def _():
            copy(j, 3).start()

        @pl.when(has_left)
        def _():
            copy(j, 4).start()

    def take_rows(j):
        copy(j, 2).wait_recv()
        target = PAD - 1 + (cz + 1) * (1 - d)
        for q in range(3):
            for x in range(cx):
                basis[j, q, x, pl.ds(target, 1), :] = rows_in[j, 0, q * cx + x : q * cx + x + 1, :]

    def take_sides(j):
        @pl.when(has_left)
        def _():
            copy(j, 0).wait_recv()
            copy(j, 3).wait_recv()

            @pl.when(d == 0)
            def _():
                left_in[j, 1, cz - 1 : cz, :] = (
                    left_in[j, 1, cz - 1 : cz, :] + rows_in[j, 1, last : last + 1, :]
                )

        @pl.when(has_right)
        def _():
            copy(j, 1).wait_recv()
            copy(j, 4).wait_recv()

            @pl.when(d == 1)
            def _():
                right_in[j, 1, PAD - 1 : PAD, :] = rows_in[j, 2, 2 * cx : 2 * cx + 1, :]

    below = pl.ds(PAD - 1, cz)
    above = pl.ds(PAD + 1, cz)

    def plane(j, x, shift):
        e0 = basis[j, 0, x, own, :]
        e1 = basis[j, 1, x, own, :]
        e2 = basis[j, 2, x, own, :]
        e0a = basis[j, 0, x, above, :]
        e1a = basis[j, 1, x, above, :]
        b1 = e1 - before(e1)
        b2 = e2 - basis[j, 2, x, below, :]
        if x == last:
            e1p = right_in[j, 0, own, :]
            e2p = right_in[j, 1, own, :]
            e2pb = right_in[j, 1, below, :]
        else:
            e1p = basis[j, 1, x + 1, own, :]
            e2p = basis[j, 2, x + 1, own, :]
            e2pb = basis[j, 2, x + 1, below, :]
        if x == 0:
            l1 = left_in[j, 0]
            l2 = left_in[j, 1]
        else:
            e0m = basis[j, 0, x - 1, own, :]
            l1 = basis[j, 1, x - 1, own, :] + (after(e0m) - e0m)
            l2 = basis[j, 2, x - 1, own, :] + (basis[j, 0, x - 1, above, :] - e0m)
        m = mass[x] + (4.0 - shift)
        g = (e1p - before(e1p)) + (e2p - e2pb) - (b1 + b2)
        q = b2 + e0
        o0 = m * e0 - (after(e0) + before(e0)) - (e0a + basis[j, 0, x, below, :]) + g
        o1 = m * e1 - (e1a + basis[j, 1, x, below, :]) - (e1p + l1) + (after(q) - q)
        o2 = (
            m * e2
            - (after(e2) + before(e2))
            - (e2p + l2)
            + ((e1a - before(e1a) + e0a) - (b1 + e0))
        )
        return o0, o1, o2

    def fold(f):
        return jnp.sum(f.reshape(cz // 8, 8, cy), axis=0)

    def finish(j, x, mode, sums):
        shift = 0.0 if mode == 0 else CENTRE
        outs = plane(j, x, shift)
        same, cross = sums
        for q in range(3):
            if mode == 0:
                new = -outs[q]
                if q == 0:
                    flat = ((s * cx + x) * (2 * cz) + z_start + row) * cy + lane
                    new = new + jnp.where(flat == cell_ref[0], SOURCE_AMP, 0.0)
            else:
                old = basis[j, q, x, own, :]
                if mode == 1:
                    new = (1.0 / HALF) * outs[q]
                else:
                    new = (2.0 / HALF) * outs[q] - basis[j - 1, q, x, own, :]
                cross = cross + fold(new * old)
            basis[j + 1, q, x, own, :] = new
            same = same + fold(new * new)
        return same, cross

    zero_sum = jnp.zeros((8, cy), jnp.float32)

    def step(j, mode, final):
        sums = (zero_sum, zero_sum)
        take_rows(j)
        for x in range(1, last):
            sums = finish(j, x, mode, sums)
        take_sides(j)
        sums = finish(j, last, mode, sums)
        if not final:
            send_right(j + 1)
        sums = finish(j, 0, mode, sums)
        if not final:
            send_left(j + 1)
            send_rows(j + 1)
        if mode == 0:
            dots[0] = sums[0]
        else:
            dots[2 * j - 1] = sums[1]
            dots[2 * j] = sums[0]

    load.wait()
    pl.semaphore_wait(barrier, group - 1 + n_src - 1)
    send_right(0)
    send_left(0)
    send_rows(0)
    step(0, 0, False)
    step(1, 1, False)

    def middle(j, carry):
        step(j, 2, False)
        return carry

    lax.fori_loop(2, DEGREE, middle, 0)
    step(DEGREE, 2, True)

    for k in range(2 * DEGREE + 1, 16):
        dots[k] = zero_sum
    mine = jnp.sum(dots[...], axis=1)
    dots_out[...] = mine

    def dot_copy(k):
        return pltpu.make_async_remote_copy(
            src_ref=dots_out,
            dst_ref=dots_in.at[k],
            send_sem=dot_send.at[k],
            recv_sem=dot_recv.at[k],
            device_id=member(k),
            device_id_type=MESH,
        )

    def dot_start(k, carry):
        dot_copy(k).start()
        return carry

    def dot_take(k, total):
        dot_copy(k).wait_recv()
        return total + dots_in[k]

    lax.fori_loop(1, group, dot_start, 0)
    total = lax.fori_loop(1, group, dot_take, mine)
    total = jnp.broadcast_to(jnp.sum(total, axis=1, keepdims=True), (16, cy))
    moments = [total[0:1]]
    for k in range(1, 2 * DEGREE + 1):
        if k % 2:
            value = total[k : k + 1]
            moments.append(value if k == 1 else 2.0 * value - moments[1])
        else:
            moments.append(2.0 * total[k : k + 1] - moments[0])
    coefficients = field_coefficients(moments)

    partial = []
    for x in range(cx):
        amount = None
        for q in range(3):
            value = basis[0, q, x, own, :]
            for k, weight in enumerate(coefficients):
                value = value + weight * basis[k + 1, q, x, own, :]
            out_ref[0, q, x] = value
            term = value * adj_ref[0, q, x]
            amount = term if amount is None else amount + term
        partial.append(amount)

    def packed(target):
        planes = []
        for a in range(cx // n_src):
            whole = None
            for b in range(n_src):
                moved = pltpu.roll(
                    partial[a * n_src + b], lax.rem((b - target + n_src) * share, cy), 1
                )
                keep = (lane >= b * share) & (lane < (b + 1) * share)
                whole = jnp.where(keep, moved, 0.0 if whole is None else whole)
            planes.append(whole)
        return planes

    def share_copy(k):
        return pltpu.make_async_remote_copy(
            src_ref=share_out.at[k],
            dst_ref=share_in.at[k],
            send_sem=share_send.at[k],
            recv_sem=share_recv.at[k],
            device_id=source(k),
            device_id_type=MESH,
        )

    for k in range(1, n_src):
        for a, value in enumerate(packed(lax.rem(c + k, n_src))):
            share_out[k, a] = value
        share_copy(k).start()
    summed = packed(c)
    for k in range(1, n_src):
        share_copy(k).wait_recv()
        summed = [value + share_in[k, a] for a, value in enumerate(summed)]
    for x in range(cx):
        a, b = divmod(x, n_src)
        scale = jnp.where(earth(x), -mass[x], 0.0)
        scale = pltpu.roll(scale, lax.rem((n_src - c) * share, cy), 1)
        value = summed[a] if b == 0 else pltpu.roll(summed[a], cy - b * share, 1)
        grad_ref[x] = (scale * value)[:, :share]

    def dot_drain(k, carry):
        dot_copy(k).wait_send()
        return carry

    lax.fori_loop(1, group, dot_drain, 0)
    for k in range(1, n_src):
        share_copy(k).wait_send()

    def drain(j, carry):
        copy(j, 2).wait_send()

        @pl.when(has_right)
        def _():
            copy(j, 0).wait_send()
            copy(j, 3).wait_send()

        @pl.when(has_left)
        def _():
            copy(j, 1).wait_send()
            copy(j, 4).wait_send()

        return carry

    lax.fori_loop(0, APPLIES, drain, 0)


def local(n_space, n_src, start_fields, adjoint_fields, conductivity, surface_rows, source_cells):
    _, _, cx, cz, cy = start_fields.shape
    group = n_space * 2
    f32 = jnp.float32
    vmem = pl.BlockSpec(memory_space=pltpu.VMEM)
    return pl.pallas_call(
        functools.partial(kernel, (n_space, n_src, cx, cz, cy)),
        out_shape=(
            jax.ShapeDtypeStruct(start_fields.shape, f32),
            jax.ShapeDtypeStruct((cx, cz, cy // n_src), f32),
        ),
        in_specs=[
            pl.BlockSpec(memory_space=pl.ANY),
            vmem,
            vmem,
            vmem,
            pl.BlockSpec(memory_space=pltpu.SMEM),
        ],
        out_specs=(vmem, vmem),
        scratch_shapes=[
            pltpu.VMEM((APPLIES + 1, 3, cx, cz + 2 * PAD, cy), f32),
            pltpu.VMEM((APPLIES, 2, cz + 2 * PAD, cy), f32),
            pltpu.VMEM((APPLIES, 2, cz, cy), f32),
            pltpu.VMEM((APPLIES, 2, cz, cy), f32),
            pltpu.VMEM((APPLIES, 16, cy), f32),
            pltpu.VMEM((APPLIES, 3, 16, cy), f32),
            pltpu.VMEM((cx, cz, cy), f32),
            pltpu.VMEM((16, 8, cy), f32),
            pltpu.VMEM((16, cy), f32),
            pltpu.VMEM((group, 16, cy), f32),
            pltpu.VMEM((n_src, cx // n_src, cz, cy), f32),
            pltpu.VMEM((n_src, cx // n_src, cz, cy), f32),
            pltpu.SemaphoreType.DMA,
            pltpu.SemaphoreType.DMA((APPLIES, 5)),
            pltpu.SemaphoreType.DMA((APPLIES, 5)),
            pltpu.SemaphoreType.DMA((group,)),
            pltpu.SemaphoreType.DMA((group,)),
            pltpu.SemaphoreType.DMA((n_src,)),
            pltpu.SemaphoreType.DMA((n_src,)),
        ],
        compiler_params=pltpu.CompilerParams(
            collective_id=0, has_side_effects=True, vmem_limit_bytes=40 * 1024 * 1024
        ),
    )(start_fields, adjoint_fields, conductivity, surface_rows, source_cells)


def solution(mesh):
    fields = P(("parts", "src"), None, "space", "depth", None)
    return jax.shard_map(
        functools.partial(local, mesh.shape["space"], mesh.shape["src"]),
        mesh=mesh,
        in_specs=(
            fields,
            fields,
            P(("parts", "space"), "depth", None),
            P(("parts", "space"), None),
            P(("parts", "src")),
        ),
        out_specs=(fields, P(("parts", "space"), "depth", "src")),
        check_vma=False,
    )
```

```python
import functools

import jax
import jax.numpy as jnp
from jax import lax
from jax.experimental import pallas as pl
from jax.experimental.pallas import tpu as pltpu
from jax.sharding import PartitionSpec as P

ITERS = 3
ALPHA = 2.0
AIR = 0.01
SOURCE_AMP = 10.0
CENTRE = 6.5
HALF = 6.5
DEGREE = 2 * ITERS
APPLIES = DEGREE + 1
PAD = 8
MESH = pl.DeviceIdType.MESH


def times_operator(poly):
    out = [None] * (len(poly) + 1)

    def add(k, term):
        out[k] = term if out[k] is None else out[k] + term

    for k, c in enumerate(poly):
        add(k, CENTRE * c)
        if k == 0:
            add(1, HALF * c)
        else:
            add(k + 1, (0.5 * HALF) * c)
            add(k - 1, (0.5 * HALF) * c)
    return out


def axpy(a, scale, b):
    out = []
    for k in range(max(len(a), len(b))):
        if k >= len(b):
            out.append(a[k])
        elif k >= len(a):
            out.append(scale * b[k])
        else:
            out.append(a[k] + scale * b[k])
    return out


def with_first(poly, moments):
    total = poly[0] * moments[0]
    for k in range(1, len(poly)):
        total = total + poly[k] * moments[k]
    return total


def inner(a, b, moments):
    total = None
    for i, u in enumerate(a):
        row = None
        for j, w in enumerate(b):
            term = w * (0.5 * (moments[i + j] + moments[abs(i - j)]))
            row = term if row is None else row + term
        total = u * row if total is None else total + u * row
    return total


def field_coefficients(moments):
    one = jnp.ones_like(moments[0])
    r = [one]
    p = [one]
    rho = moments[0]
    x = []
    for step in range(ITERS):
        v = times_operator(p)
        alpha = rho / with_first(v, moments)
        s = axpy(r, -alpha, v)
        t = times_operator(s)
        omega = inner(t, s, moments) / inner(t, t, moments)
        x = axpy(axpy(x, alpha, p), omega, s)
        if step + 1 < ITERS:
            r = axpy(s, -omega, t)
            rho_new = with_first(r, moments)
            beta = rho_new / rho * (alpha / omega)
            p = axpy(r, beta, axpy(p, -omega, v))
            rho = rho_new
    return x


def kernel(
    sizes,
    start_ref,
    adj_ref,
    cond_ref,
    surf_ref,
    cell_ref,
    out_ref,
    grad_ref,
    basis,
    right_in,
    left_in,
    left_out,
    rows_out,
    rows_in,
    mass,
    adj,
    cond,
    surf,
    cell,
    dots,
    dots_in,
    weights,
    share_out,
    share_in,
    load_sem,
    send_sem,
    recv_sem,
    dot_send,
    dot_recv,
    share_send,
    share_recv,
):
    n_space, n_src, cx, cz, cy = sizes
    group = n_space * 2
    everyone = group * n_src
    share = cy // n_src
    last = cx - 1
    s = lax.axis_index("space")
    d = lax.axis_index("depth")
    c = lax.axis_index("src")
    me = c * group + s * 2 + d

    def member(g):
        return {"src": g // group, "space": lax.rem(g, group) // 2, "depth": lax.rem(g, 2)}

    def other(k):
        return lax.rem(me + k, everyone)

    def source(k):
        return {"src": lax.rem(c + k, n_src)}

    own = pl.ds(PAD, cz)
    load = pltpu.make_async_copy(start_ref.at[0], basis.at[0, :, :, own, :], load_sem.at[0])
    load.start()
    barrier = pltpu.get_barrier_semaphore()

    def greet(k, carry):
        pl.semaphore_signal(barrier, inc=1, device_id=member(other(k)), device_id_type=MESH)
        return carry

    lax.fori_loop(1, everyone, greet, 0)
    load_cond = pltpu.make_async_copy(cond_ref, cond, load_sem.at[1])
    load_surf = pltpu.make_async_copy(surf_ref, surf, load_sem.at[2])
    load_cell = pltpu.make_async_copy(cell_ref, cell, load_sem.at[3])
    load_adj = pltpu.make_async_copy(adj_ref.at[0], adj, load_sem.at[4])
    load_surf.start()
    load_cond.start()
    load_cell.start()
    load_adj.start()

    lane = lax.broadcasted_iota(jnp.int32, (cz, cy), 1)
    row = lax.broadcasted_iota(jnp.int32, (cz, cy), 0)
    first_lane = lane == 0
    last_lane = lane == cy - 1
    z_start = d * cz
    zero_row = jnp.zeros((1, cy), jnp.float32)

    def earth(x):
        return (z_start + row) >= surf[pl.ds(x, 1), :]

    zero_rows = jnp.zeros((3, cx, 1, cy), jnp.float32)

    def clear(j, carry):
        basis[j, :, :, PAD - 1 : PAD, :] = zero_rows
        basis[j, :, :, PAD + cz : PAD + cz + 1, :] = zero_rows
        right_in[j, 1, PAD - 1 : PAD, :] = zero_row
        rows_out[j] = jnp.zeros((16, cy), jnp.float32)
        return carry

    lax.fori_loop(0, APPLIES, clear, 0)

    @pl.when(s == 0)
    def _():
        left_in[...] = jnp.zeros(left_in.shape, jnp.float32)

    @pl.when(s == n_space - 1)
    def _():
        def blank(j, carry):
            right_in[j, :, own, :] = jnp.zeros((2, cz, cy), jnp.float32)
            return carry

        lax.fori_loop(0, APPLIES, blank, 0)

    def before(f):
        return jnp.where(first_lane, 0.0, pltpu.roll(f, 1, 1))

    def after(f):
        return jnp.where(last_lane, 0.0, pltpu.roll(f, cy - 1, 1))

    def copy(j, kind):
        if kind == 0:
            src, dst, where = left_out.at[j], left_in.at[j], {"space": s + 1}
        elif kind == 1:
            src = basis.at[j, pl.ds(1, 2), 0, own, :]
            dst, where = right_in.at[j, :, own, :], {"space": s - 1}
        else:
            src, dst = rows_out.at[j], rows_in.at[j, kind - 2]
            where = {"depth": 1 - d}
            if kind == 3:
                where["space"] = s + 1
            elif kind == 4:
                where["space"] = s - 1
        return pltpu.make_async_remote_copy(
            src_ref=src,
            dst_ref=dst,
            send_sem=send_sem.at[j, kind],
            recv_sem=recv_sem.at[j, kind],
            device_id=where,
            device_id_type=MESH,
        )

    has_left = s > 0
    has_right = s < n_space - 1

    def send_right(j):
        e0 = basis[j, 0, last, own, :]
        left_out[j, 0] = basis[j, 1, last, own, :] + after(e0) - e0
        left_out[j, 1] = basis[j, 2, last, own, :] + basis[j, 0, last, pl.ds(PAD + 1, cz), :] - e0

        @pl.when(has_right)
        def _():
            copy(j, 0).start()

    def send_left(j):
        @pl.when(has_left)
        def _():
            copy(j, 1).start()

    edge = PAD + (cz - 1) * (1 - d)

    def send_rows(j):
        for q in range(3):
            for x in range(cx):
                rows_out[j, q * cx + x : q * cx + x + 1, :] = basis[j, q, x, pl.ds(edge, 1), :]
        copy(j, 2).start()

        @pl.when(has_right)
        def _():
            copy(j, 3).start()

        @pl.when(has_left)
        def _():
            copy(j, 4).start()

    def take_rows(j):
        copy(j, 2).wait_recv()
        target = PAD - 1 + (cz + 1) * (1 - d)
        for q in range(3):
            for x in range(cx):
                basis[j, q, x, pl.ds(target, 1), :] = rows_in[j, 0, q * cx + x : q * cx + x + 1, :]

    def take_left(j):
        @pl.when(has_left)
        def _():
            copy(j, 3).wait_recv()
            copy(j, 0).wait_recv()

            @pl.when(d == 0)
            def _():
                left_in[j, 1, cz - 1 : cz, :] = (
                    left_in[j, 1, cz - 1 : cz, :] + rows_in[j, 1, last : last + 1, :]
                )

    def take_right(j):
        @pl.when(has_right)
        def _():
            copy(j, 4).wait_recv()
            copy(j, 1).wait_recv()

            @pl.when(d == 1)
            def _():
                right_in[j, 1, PAD - 1 : PAD, :] = rows_in[j, 2, 2 * cx : 2 * cx + 1, :]

    below = pl.ds(PAD - 1, cz)
    above = pl.ds(PAD + 1, cz)

    def plane(j, x, shift):
        e0 = basis[j, 0, x, own, :]
        e1 = basis[j, 1, x, own, :]
        e2 = basis[j, 2, x, own, :]
        e0a = basis[j, 0, x, above, :]
        e1a = basis[j, 1, x, above, :]
        b1 = e1 - before(e1)
        b2 = e2 - basis[j, 2, x, below, :]
        if x == last:
            e1p = right_in[j, 0, own, :]
            e2p = right_in[j, 1, own, :]
            e2pb = right_in[j, 1, below, :]
        else:
            e1p = basis[j, 1, x + 1, own, :]
            e2p = basis[j, 2, x + 1, own, :]
            e2pb = basis[j, 2, x + 1, below, :]
        if x == 0:
            l1 = left_in[j, 0]
            l2 = left_in[j, 1]
        else:
            e0m = basis[j, 0, x - 1, own, :]
            l1 = basis[j, 1, x - 1, own, :] + (after(e0m) - e0m)
            l2 = basis[j, 2, x - 1, own, :] + (basis[j, 0, x - 1, above, :] - e0m)
        m = mass[x] + (4.0 - shift)
        g = (e1p - before(e1p)) + (e2p - e2pb) - (b1 + b2)
        q = b2 + e0
        o0 = m * e0 - (after(e0) + before(e0)) - (e0a + basis[j, 0, x, below, :]) + g
        o1 = m * e1 - (e1a + basis[j, 1, x, below, :]) - (e1p + l1) + (after(q) - q)
        o2 = (
            m * e2
            - (after(e2) + before(e2))
            - (e2p + l2)
            + ((e1a - before(e1a) + e0a) - (b1 + e0))
        )
        return o0, o1, o2

    def fold(f):
        return jnp.sum(f.reshape(cz // 8, 8, cy), axis=0)

    def finish(j, x, mode, sums):
        shift = 0.0 if mode == 0 else CENTRE
        outs = plane(j, x, shift)
        same, cross = sums
        for q in range(3):
            if mode == 0:
                new = -outs[q]
                if q == 0:
                    flat = ((s * cx + x) * (2 * cz) + z_start + row) * cy + lane
                    new = new + jnp.where(flat == cell[0], SOURCE_AMP, 0.0)
            else:
                old = basis[j, q, x, own, :]
                if mode == 1:
                    new = (1.0 / HALF) * outs[q]
                else:
                    new = (2.0 / HALF) * outs[q] - basis[j - 1, q, x, own, :]
                cross = cross + fold(new * old)
            basis[j + 1, q, x, own, :] = new
            same = same + fold(new * new)
        return same, cross

    zero_sum = jnp.zeros((8, cy), jnp.float32)

    def packed(planes, target):
        out = []
        for a in range(cx // n_src):
            whole = None
            for b in range(n_src):
                moved = pltpu.roll(
                    planes[a * n_src + b], lax.rem((b - target + n_src) * share, cy), 1
                )
                keep = (lane >= b * share) & (lane < (b + 1) * share)
                whole = moved if b == 0 else jnp.where(keep, moved, whole)
            out.append(whole)
        return out

    def share_copy(e, k):
        return pltpu.make_async_remote_copy(
            src_ref=share_out.at[e, k],
            dst_ref=share_in.at[e, k],
            send_sem=share_send.at[e, k],
            recv_sem=share_recv.at[e, k],
            device_id=source(k),
            device_id_type=MESH,
        )

    def send_shares(e):
        planes = []
        for x in range(cx):
            amount = basis[e, 0, x, own, :] * adj[0, x]
            for q in range(1, 3):
                amount = amount + basis[e, q, x, own, :] * adj[q, x]
            planes.append(amount)
        for k in range(n_src):
            for a, value in enumerate(packed(planes, lax.rem(c + k, n_src))):
                share_out[e, k, a] = value
            if k:
                share_copy(e, k).start()

    def step(j, mode, final, right_first):
        sums = (zero_sum, zero_sum)
        take_rows(j)
        for x in range(1, last):
            sums = finish(j, x, mode, sums)
        for right in (right_first, not right_first):
            if right:
                take_right(j)
                sums = finish(j, last, mode, sums)
                if not final:
                    send_right(j + 1)
            else:
                take_left(j)
                sums = finish(j, 0, mode, sums)
                if not final:
                    send_left(j + 1)
        if not final:
            send_rows(j + 1)
            send_shares(j + 1)
        if mode == 0:
            dots[0] = sums[0]
        else:
            dots[2 * j - 1] = sums[1]
            dots[2 * j] = sums[0]

    load.wait()
    pl.semaphore_wait(barrier, everyone - 1)
    send_right(0)
    send_left(0)
    send_rows(0)
    load_surf.wait()
    load_cond.wait()
    load_cell.wait()
    for x in range(cx):
        mass[x] = ALPHA * jnp.where(earth(x), cond[x], AIR)
    load_adj.wait()
    send_shares(0)
    step(0, 0, False, False)
    step(1, 1, False, True)

    def middle(i, carry):
        step(2 * i, 2, False, False)
        step(2 * i + 1, 2, False, True)
        return carry

    lax.fori_loop(1, ITERS, middle, 0)
    step(DEGREE, 2, True, False)

    count = 2 * DEGREE + 1
    for k in range(count, 16):
        dots[k] = zero_sum
    mine = jnp.sum(jnp.sum(dots[...], axis=1), axis=1, keepdims=True)
    diagonal = lax.broadcasted_iota(jnp.int32, (16, cy), 0) == lax.broadcasted_iota(
        jnp.int32, (16, cy), 1
    )
    dots_in[me] = jnp.sum(jnp.where(diagonal, mine, 0.0), axis=0, keepdims=True)

    def dot_copy(slot, k):
        return pltpu.make_async_remote_copy(
            src_ref=dots_in.at[slot],
            dst_ref=dots_in.at[slot],
            send_sem=dot_send.at[k],
            recv_sem=dot_recv.at[slot],
            device_id=member(other(k)),
            device_id_type=MESH,
        )

    def dot_start(k, carry):
        dot_copy(me, k).start()
        return carry

    def dot_take(k, carry):
        dot_copy(other(k), k).wait_recv()
        return carry

    lax.fori_loop(1, everyone, dot_start, 0)
    lax.fori_loop(1, everyone, dot_take, 0)
    table = None
    source_row = lax.broadcasted_iota(jnp.int32, (8, cy), 0)
    for q in range(n_src):
        total = dots_in[q * group]
        for g in range(1, group):
            total = total + dots_in[q * group + g]
        total = jnp.broadcast_to(total, (8, cy))
        table = total if q == 0 else jnp.where(source_row == q, total, table)
    moments = []
    for k in range(count):
        value = jnp.broadcast_to(table[:, k : k + 1], (8, cy))
        moments.append(value if k < 2 else 2.0 * value - moments[k % 2])
    for k, value in enumerate(field_coefficients(moments)):
        weights[k] = value

    coefficients = [weights[k, pl.ds(c, 1), :] for k in range(DEGREE)]
    for x in range(cx):
        for q in range(3):
            value = basis[0, q, x, own, :]
            for k, weight in enumerate(coefficients):
                value = value + weight * basis[k + 1, q, x, own, :]
            out_ref[0, q, x] = value
    for e in range(DEGREE + 1):
        for k in range(1, n_src):
            share_copy(e, k).wait_recv()
    summed = []
    for a in range(cx // n_src):
        value = None
        for k in range(n_src):
            origin = lax.rem(c + n_src - k, n_src)
            held = share_in if k else share_out
            term = held[0, k, a]
            value = term if value is None else value + term
            for e in range(DEGREE):
                value = value + weights[e, pl.ds(origin, 1), :] * held[e + 1, k, a]
        summed.append(value)
    for x in range(cx):
        a, b = divmod(x, n_src)
        scale = jnp.where(earth(x), -mass[x], 0.0)
        scale = pltpu.roll(scale, lax.rem((n_src - c) * share, cy), 1)
        value = summed[a] if b == 0 else pltpu.roll(summed[a], cy - b * share, 1)
        grad_ref[x] = (scale * value)[:, :share]

    def dot_drain(k, carry):
        dot_copy(me, k).wait_send()
        return carry

    lax.fori_loop(1, everyone, dot_drain, 0)
    for e in range(DEGREE + 1):
        for k in range(1, n_src):
            share_copy(e, k).wait_send()

    def drain(j, carry):
        copy(j, 2).wait_send()

        @pl.when(has_right)
        def _():
            copy(j, 0).wait_send()
            copy(j, 3).wait_send()

        @pl.when(has_left)
        def _():
            copy(j, 1).wait_send()
            copy(j, 4).wait_send()

        return carry

    lax.fori_loop(0, APPLIES, drain, 0)


def local(n_space, n_src, start_fields, adjoint_fields, conductivity, surface_rows, source_cells):
    _, _, cx, cz, cy = start_fields.shape
    everyone = n_space * 2 * n_src
    f32 = jnp.float32
    vmem = pl.BlockSpec(memory_space=pltpu.VMEM)
    shares = (DEGREE + 1, n_src, cx // n_src, cz, cy)
    return pl.pallas_call(
        functools.partial(kernel, (n_space, n_src, cx, cz, cy)),
        out_shape=(
            jax.ShapeDtypeStruct(start_fields.shape, f32),
            jax.ShapeDtypeStruct((cx, cz, cy // n_src), f32),
        ),
        in_specs=[pl.BlockSpec(memory_space=pltpu.HBM)] * 5,
        out_specs=(vmem, vmem),
        scratch_shapes=[
            pltpu.VMEM((APPLIES + 1, 3, cx, cz + 2 * PAD, cy), f32),
            pltpu.VMEM((APPLIES, 2, cz + 2 * PAD, cy), f32),
            pltpu.VMEM((APPLIES, 2, cz, cy), f32),
            pltpu.VMEM((APPLIES, 2, cz, cy), f32),
            pltpu.VMEM((APPLIES, 16, cy), f32),
            pltpu.VMEM((APPLIES, 3, 16, cy), f32),
            pltpu.VMEM((cx, cz, cy), f32),
            pltpu.VMEM((3, cx, cz, cy), f32),
            pltpu.VMEM((cx, cz, cy), f32),
            pltpu.VMEM((cx, cy), jnp.int32),
            pltpu.SMEM((1,), jnp.int32),
            pltpu.VMEM((16, 8, cy), f32),
            pltpu.VMEM((everyone, 1, cy), f32),
            pltpu.VMEM((DEGREE, 8, cy), f32),
            pltpu.VMEM(shares, f32),
            pltpu.VMEM(shares, f32),
            pltpu.SemaphoreType.DMA((5,)),
            pltpu.SemaphoreType.DMA((APPLIES, 5)),
            pltpu.SemaphoreType.DMA((APPLIES, 5)),
            pltpu.SemaphoreType.DMA((everyone,)),
            pltpu.SemaphoreType.DMA((everyone,)),
            pltpu.SemaphoreType.DMA((DEGREE + 1, n_src)),
            pltpu.SemaphoreType.DMA((DEGREE + 1, n_src)),
        ],
        compiler_params=pltpu.CompilerParams(
            collective_id=0, has_side_effects=True, vmem_limit_bytes=40 * 1024 * 1024
        ),
    )(start_fields, adjoint_fields, conductivity, surface_rows, source_cells)


def solution(mesh):
    fields = P(("parts", "src"), None, "space", "depth", None)
    return jax.shard_map(
        functools.partial(local, mesh.shape["space"], mesh.shape["src"]),
        mesh=mesh,
        in_specs=(
            fields,
            fields,
            P(("parts", "space"), "depth", None),
            P(("parts", "space"), None),
            P(("parts", "src")),
        ),
        out_specs=(fields, P(("parts", "space"), "depth", "src")),
        check_vma=False,
    )
```

```python
import functools

import jax
import jax.numpy as jnp
from jax import lax
from jax.experimental import pallas as pl
from jax.experimental.pallas import tpu as pltpu
from jax.sharding import PartitionSpec as P

ITERS = 3
ALPHA = 2.0
AIR = 0.01
SOURCE_AMP = 10.0
CENTRE = 6.5
HALF = 6.5
DEGREE = 2 * ITERS
APPLIES = DEGREE + 1
PAD = 8
MESH = pl.DeviceIdType.MESH


def times_operator(poly):
    out = [None] * (len(poly) + 1)

    def add(k, term):
        out[k] = term if out[k] is None else out[k] + term

    for k, c in enumerate(poly):
        add(k, CENTRE * c)
        if k == 0:
            add(1, HALF * c)
        else:
            add(k + 1, (0.5 * HALF) * c)
            add(k - 1, (0.5 * HALF) * c)
    return out


def axpy(a, scale, b):
    out = []
    for k in range(max(len(a), len(b))):
        if k >= len(b):
            out.append(a[k])
        elif k >= len(a):
            out.append(scale * b[k])
        else:
            out.append(a[k] + scale * b[k])
    return out


def with_first(poly, moments):
    total = poly[0] * moments[0]
    for k in range(1, len(poly)):
        total = total + poly[k] * moments[k]
    return total


def inner(a, b, moments):
    total = None
    for i, u in enumerate(a):
        row = None
        for j, w in enumerate(b):
            term = w * (0.5 * (moments[i + j] + moments[abs(i - j)]))
            row = term if row is None else row + term
        total = u * row if total is None else total + u * row
    return total


def field_coefficients(moments):
    one = jnp.ones_like(moments[0])
    r = [one]
    p = [one]
    rho = moments[0]
    x = []
    for step in range(ITERS):
        v = times_operator(p)
        alpha = rho / with_first(v, moments)
        s = axpy(r, -alpha, v)
        t = times_operator(s)
        omega = inner(t, s, moments) / inner(t, t, moments)
        x = axpy(axpy(x, alpha, p), omega, s)
        if step + 1 < ITERS:
            r = axpy(s, -omega, t)
            rho_new = with_first(r, moments)
            beta = rho_new / rho * (alpha / omega)
            p = axpy(r, beta, axpy(p, -omega, v))
            rho = rho_new
    return x


def kernel(
    sizes,
    start_ref,
    adj_ref,
    cond_ref,
    surf_ref,
    cell_ref,
    out_ref,
    grad_ref,
    basis,
    right_in,
    left_in,
    left_out,
    rows_out,
    rows_in,
    mass,
    adj,
    cond,
    surf,
    cell,
    dots,
    dots_in,
    weights,
    share_out,
    share_in,
    load_sem,
    send_sem,
    recv_sem,
    dot_send,
    dot_recv,
    share_send,
    share_recv,
):
    n_space, n_src, cx, cz, cy = sizes
    group = n_space * 2
    everyone = group * n_src
    share = cy // n_src
    last = cx - 1
    s = lax.axis_index("space")
    d = lax.axis_index("depth")
    c = lax.axis_index("src")
    me = c * group + s * 2 + d

    def member(g):
        return {"src": g // group, "space": lax.rem(g, group) // 2, "depth": lax.rem(g, 2)}

    def other(k):
        return lax.rem(me + k, everyone)

    def source(k):
        return {"src": lax.rem(c + k, n_src)}

    own = pl.ds(PAD, cz)
    load = pltpu.make_async_copy(start_ref.at[0], basis.at[0, :, :, own, :], load_sem.at[0])
    load.start()
    barrier = pltpu.get_barrier_semaphore()

    def greet(k, carry):
        pl.semaphore_signal(barrier, inc=1, device_id=member(other(k)), device_id_type=MESH)
        return carry

    near_only = 2 <= n_space < DEGREE
    if near_only:
        for target in [{"depth": 1 - d}] + [source(k) for k in range(1, n_src)]:
            pl.semaphore_signal(barrier, inc=1, device_id=target, device_id_type=MESH)
        for present, side in ((s > 0, s - 1), (s < n_space - 1, s + 1)):

            @pl.when(present)
            def _():
                for half in (d, 1 - d):
                    pl.semaphore_signal(
                        barrier,
                        inc=1,
                        device_id={"space": side, "depth": half},
                        device_id_type=MESH,
                    )

    else:
        lax.fori_loop(1, everyone, greet, 0)
    load_cond = pltpu.make_async_copy(cond_ref, cond, load_sem.at[1])
    load_surf = pltpu.make_async_copy(surf_ref, surf, load_sem.at[2])
    load_cell = pltpu.make_async_copy(cell_ref, cell, load_sem.at[3])
    load_adj = pltpu.make_async_copy(adj_ref.at[0], adj, load_sem.at[4])
    load_surf.start()
    load_cond.start()
    load_cell.start()
    load_adj.start()

    lane = lax.broadcasted_iota(jnp.int32, (cz, cy), 1)
    row = lax.broadcasted_iota(jnp.int32, (cz, cy), 0)
    first_lane = lane == 0
    last_lane = lane == cy - 1
    z_start = d * cz
    zero_row = jnp.zeros((1, cy), jnp.float32)

    def earth(x):
        return (z_start + row) >= surf[pl.ds(x, 1), :]

    zero_rows = jnp.zeros((3, cx, 1, cy), jnp.float32)

    def clear(j, carry):
        basis[j, :, :, PAD - 1 : PAD, :] = zero_rows
        basis[j, :, :, PAD + cz : PAD + cz + 1, :] = zero_rows
        right_in[j, 1, PAD - 1 : PAD, :] = zero_row
        rows_out[j] = jnp.zeros((16, cy), jnp.float32)
        return carry

    lax.fori_loop(0, APPLIES, clear, 0)

    @pl.when(s == 0)
    def _():
        left_in[...] = jnp.zeros(left_in.shape, jnp.float32)

    @pl.when(s == n_space - 1)
    def _():
        def blank(j, carry):
            right_in[j, :, own, :] = jnp.zeros((2, cz, cy), jnp.float32)
            return carry

        lax.fori_loop(0, APPLIES, blank, 0)

    def before(f):
        return jnp.where(first_lane, 0.0, pltpu.roll(f, 1, 1))

    def after(f):
        return jnp.where(last_lane, 0.0, pltpu.roll(f, cy - 1, 1))

    def copy(j, kind):
        if kind == 0:
            src, dst, where = left_out.at[j], left_in.at[j], {"space": s + 1}
        elif kind == 1:
            src = basis.at[j, pl.ds(1, 2), 0, own, :]
            dst, where = right_in.at[j, :, own, :], {"space": s - 1}
        else:
            src, dst = rows_out.at[j], rows_in.at[j, kind - 2]
            where = {"depth": 1 - d}
            if kind == 3:
                where["space"] = s + 1
            elif kind == 4:
                where["space"] = s - 1
        return pltpu.make_async_remote_copy(
            src_ref=src,
            dst_ref=dst,
            send_sem=send_sem.at[j, kind],
            recv_sem=recv_sem.at[j, kind],
            device_id=where,
            device_id_type=MESH,
        )

    has_left = s > 0
    has_right = s < n_space - 1

    def send_right(j):
        e0 = basis[j, 0, last, own, :]
        left_out[j, 0] = basis[j, 1, last, own, :] + after(e0) - e0
        left_out[j, 1] = basis[j, 2, last, own, :] + basis[j, 0, last, pl.ds(PAD + 1, cz), :] - e0

        @pl.when(has_right)
        def _():
            copy(j, 0).start()

    def send_left(j):
        @pl.when(has_left)
        def _():
            copy(j, 1).start()

    edge = PAD + (cz - 1) * (1 - d)

    def send_rows(j):
        for q in range(3):
            for x in range(cx):
                rows_out[j, q * cx + x : q * cx + x + 1, :] = basis[j, q, x, pl.ds(edge, 1), :]
        copy(j, 2).start()

        @pl.when(has_right)
        def _():
            copy(j, 3).start()

        @pl.when(has_left)
        def _():
            copy(j, 4).start()

    def take_rows(j):
        copy(j, 2).wait_recv()
        target = PAD - 1 + (cz + 1) * (1 - d)
        for q in range(3):
            for x in range(cx):
                basis[j, q, x, pl.ds(target, 1), :] = rows_in[j, 0, q * cx + x : q * cx + x + 1, :]

    def take_left(j):
        @pl.when(has_left)
        def _():
            copy(j, 3).wait_recv()
            copy(j, 0).wait_recv()

            @pl.when(d == 0)
            def _():
                left_in[j, 1, cz - 1 : cz, :] = (
                    left_in[j, 1, cz - 1 : cz, :] + rows_in[j, 1, last : last + 1, :]
                )

    def take_right(j):
        @pl.when(has_right)
        def _():
            copy(j, 4).wait_recv()
            copy(j, 1).wait_recv()

            @pl.when(d == 1)
            def _():
                right_in[j, 1, PAD - 1 : PAD, :] = rows_in[j, 2, 2 * cx : 2 * cx + 1, :]

    below = pl.ds(PAD - 1, cz)
    above = pl.ds(PAD + 1, cz)

    def plane(j, x, shift):
        e0 = basis[j, 0, x, own, :]
        e1 = basis[j, 1, x, own, :]
        e2 = basis[j, 2, x, own, :]
        e0a = basis[j, 0, x, above, :]
        e1a = basis[j, 1, x, above, :]
        b1 = e1 - before(e1)
        b2 = e2 - basis[j, 2, x, below, :]
        if x == last:
            e1p = right_in[j, 0, own, :]
            e2p = right_in[j, 1, own, :]
            e2pb = right_in[j, 1, below, :]
        else:
            e1p = basis[j, 1, x + 1, own, :]
            e2p = basis[j, 2, x + 1, own, :]
            e2pb = basis[j, 2, x + 1, below, :]
        if x == 0:
            l1 = left_in[j, 0]
            l2 = left_in[j, 1]
        else:
            e0m = basis[j, 0, x - 1, own, :]
            l1 = basis[j, 1, x - 1, own, :] + (after(e0m) - e0m)
            l2 = basis[j, 2, x - 1, own, :] + (basis[j, 0, x - 1, above, :] - e0m)
        m = mass[x] + (4.0 - shift)
        g = (e1p - before(e1p)) + (e2p - e2pb) - (b1 + b2)
        q = b2 + e0
        o0 = m * e0 - (after(e0) + before(e0)) - (e0a + basis[j, 0, x, below, :]) + g
        o1 = m * e1 - (e1a + basis[j, 1, x, below, :]) - (e1p + l1) + (after(q) - q)
        o2 = (
            m * e2
            - (after(e2) + before(e2))
            - (e2p + l2)
            + ((e1a - before(e1a) + e0a) - (b1 + e0))
        )
        return o0, o1, o2

    def fold(f):
        return jnp.sum(f.reshape(cz // 8, 8, cy), axis=0)

    def finish(j, x, mode, sums):
        shift = 0.0 if mode == 0 else CENTRE
        outs = plane(j, x, shift)
        same, cross = sums
        for q in range(3):
            if mode == 0:
                new = -outs[q]
                if q == 0:
                    flat = ((s * cx + x) * (2 * cz) + z_start + row) * cy + lane
                    new = new + jnp.where(flat == cell[0], SOURCE_AMP, 0.0)
            else:
                old = basis[j, q, x, own, :]
                if mode == 1:
                    new = (1.0 / HALF) * outs[q]
                else:
                    new = (2.0 / HALF) * outs[q] - basis[j - 1, q, x, own, :]
                cross = cross + fold(new * old)
            basis[j + 1, q, x, own, :] = new
            same = same + fold(new * new)
        return same, cross

    zero_sum = jnp.zeros((8, cy), jnp.float32)

    def packed(planes, target):
        out = []
        for a in range(cx // n_src):
            whole = None
            for b in range(n_src):
                moved = pltpu.roll(
                    planes[a * n_src + b], lax.rem((b - target + n_src) * share, cy), 1
                )
                keep = (lane >= b * share) & (lane < (b + 1) * share)
                whole = moved if b == 0 else jnp.where(keep, moved, whole)
            out.append(whole)
        return out

    def share_copy(e, k):
        return pltpu.make_async_remote_copy(
            src_ref=share_out.at[e, k],
            dst_ref=share_in.at[e, k],
            send_sem=share_send.at[e, k],
            recv_sem=share_recv.at[e, k],
            device_id=source(k),
            device_id_type=MESH,
        )

    def send_shares(e):
        planes = []
        for x in range(cx):
            amount = basis[e, 0, x, own, :] * adj[0, x]
            for q in range(1, 3):
                amount = amount + basis[e, q, x, own, :] * adj[q, x]
            planes.append(amount)
        for k in range(n_src):
            for a, value in enumerate(packed(planes, lax.rem(c + k, n_src))):
                share_out[e, k, a] = value
            if k:
                share_copy(e, k).start()

    def step(j, mode, final, right_first):
        sums = (zero_sum, zero_sum)
        take_rows(j)
        for x in range(1, last):
            sums = finish(j, x, mode, sums)
        for right in (right_first, not right_first):
            if right:
                take_right(j)
                sums = finish(j, last, mode, sums)
                if not final:
                    send_right(j + 1)
            else:
                take_left(j)
                sums = finish(j, 0, mode, sums)
                if not final:
                    send_left(j + 1)
        if not final:
            send_rows(j + 1)
            send_shares(j + 1)
        if mode == 0:
            dots[0] = sums[0]
        else:
            dots[2 * j - 1] = sums[1]
            dots[2 * j] = sums[0]

    load.wait()
    if near_only:
        inside = has_left & has_right

        @pl.when(inside)
        def _():
            pl.semaphore_wait(barrier, n_src + 4)

        @pl.when(jnp.logical_not(inside))
        def _():
            pl.semaphore_wait(barrier, n_src + 2)

    else:
        pl.semaphore_wait(barrier, everyone - 1)
    send_right(0)
    send_left(0)
    send_rows(0)
    load_surf.wait()
    load_cond.wait()
    load_cell.wait()
    for x in range(cx):
        mass[x] = ALPHA * jnp.where(earth(x), cond[x], AIR)
    load_adj.wait()
    send_shares(0)
    step(0, 0, False, False)
    step(1, 1, False, True)

    def middle(i, carry):
        step(2 * i, 2, False, False)
        step(2 * i + 1, 2, False, True)
        return carry

    lax.fori_loop(1, ITERS, middle, 0)
    step(DEGREE, 2, True, False)

    count = 2 * DEGREE + 1
    for k in range(count, 16):
        dots[k] = zero_sum
    mine = jnp.sum(jnp.sum(dots[...], axis=1), axis=1, keepdims=True)
    diagonal = lax.broadcasted_iota(jnp.int32, (16, cy), 0) == lax.broadcasted_iota(
        jnp.int32, (16, cy), 1
    )
    dots_in[me] = jnp.sum(jnp.where(diagonal, mine, 0.0), axis=0, keepdims=True)

    def dot_copy(slot, k):
        return pltpu.make_async_remote_copy(
            src_ref=dots_in.at[slot],
            dst_ref=dots_in.at[slot],
            send_sem=dot_send.at[k],
            recv_sem=dot_recv.at[slot],
            device_id=member(other(k)),
            device_id_type=MESH,
        )

    def dot_start(k, carry):
        dot_copy(me, k).start()
        return carry

    def dot_take(k, carry):
        dot_copy(other(k), k).wait_recv()
        return carry

    for e in range(DEGREE + 1):
        for k in range(1, n_src):
            share_copy(e, k).wait_recv()
    lax.fori_loop(1, everyone, dot_start, 0)
    lax.fori_loop(1, everyone, dot_take, 0)
    table = None
    source_row = lax.broadcasted_iota(jnp.int32, (8, cy), 0)
    for q in range(n_src):
        total = dots_in[q * group]
        for g in range(1, group):
            total = total + dots_in[q * group + g]
        total = jnp.broadcast_to(total, (8, cy))
        table = total if q == 0 else jnp.where(source_row == q, total, table)
    moments = []
    for k in range(count):
        value = jnp.broadcast_to(table[:, k : k + 1], (8, cy))
        moments.append(value if k < 2 else 2.0 * value - moments[k % 2])
    for k, value in enumerate(field_coefficients(moments)):
        weights[k] = value

    coefficients = [weights[k, pl.ds(c, 1), :] for k in range(DEGREE)]
    for x in range(cx):
        for q in range(3):
            value = basis[0, q, x, own, :]
            for k, weight in enumerate(coefficients):
                value = value + weight * basis[k + 1, q, x, own, :]
            out_ref[0, q, x] = value
    summed = []
    for a in range(cx // n_src):
        value = None
        for k in range(n_src):
            origin = lax.rem(c + n_src - k, n_src)
            held = share_in if k else share_out
            term = held[0, k, a]
            value = term if value is None else value + term
            for e in range(DEGREE):
                value = value + weights[e, pl.ds(origin, 1), :] * held[e + 1, k, a]
        summed.append(value)
    for x in range(cx):
        a, b = divmod(x, n_src)
        scale = jnp.where(earth(x), -mass[x], 0.0)
        scale = pltpu.roll(scale, lax.rem((n_src - c) * share, cy), 1)
        value = summed[a] if b == 0 else pltpu.roll(summed[a], cy - b * share, 1)
        grad_ref[x] = (scale * value)[:, :share]

    def dot_drain(k, carry):
        dot_copy(me, k).wait_send()
        return carry

    lax.fori_loop(1, everyone, dot_drain, 0)
    for e in range(DEGREE + 1):
        for k in range(1, n_src):
            share_copy(e, k).wait_send()

    def drain(j, carry):
        copy(j, 2).wait_send()

        @pl.when(has_right)
        def _():
            copy(j, 0).wait_send()
            copy(j, 3).wait_send()

        @pl.when(has_left)
        def _():
            copy(j, 1).wait_send()
            copy(j, 4).wait_send()

        return carry

    lax.fori_loop(0, APPLIES, drain, 0)


def local(n_space, n_src, start_fields, adjoint_fields, conductivity, surface_rows, source_cells):
    _, _, cx, cz, cy = start_fields.shape
    everyone = n_space * 2 * n_src
    f32 = jnp.float32
    vmem = pl.BlockSpec(memory_space=pltpu.VMEM)
    shares = (DEGREE + 1, n_src, cx // n_src, cz, cy)
    return pl.pallas_call(
        functools.partial(kernel, (n_space, n_src, cx, cz, cy)),
        out_shape=(
            jax.ShapeDtypeStruct(start_fields.shape, f32),
            jax.ShapeDtypeStruct((cx, cz, cy // n_src), f32),
        ),
        in_specs=[pl.BlockSpec(memory_space=pltpu.HBM)] * 5,
        out_specs=(vmem, vmem),
        scratch_shapes=[
            pltpu.VMEM((APPLIES + 1, 3, cx, cz + 2 * PAD, cy), f32),
            pltpu.VMEM((APPLIES, 2, cz + 2 * PAD, cy), f32),
            pltpu.VMEM((APPLIES, 2, cz, cy), f32),
            pltpu.VMEM((APPLIES, 2, cz, cy), f32),
            pltpu.VMEM((APPLIES, 16, cy), f32),
            pltpu.VMEM((APPLIES, 3, 16, cy), f32),
            pltpu.VMEM((cx, cz, cy), f32),
            pltpu.VMEM((3, cx, cz, cy), f32),
            pltpu.VMEM((cx, cz, cy), f32),
            pltpu.VMEM((cx, cy), jnp.int32),
            pltpu.SMEM((1,), jnp.int32),
            pltpu.VMEM((16, 8, cy), f32),
            pltpu.VMEM((everyone, 1, cy), f32),
            pltpu.VMEM((DEGREE, 8, cy), f32),
            pltpu.VMEM(shares, f32),
            pltpu.VMEM(shares, f32),
            pltpu.SemaphoreType.DMA((5,)),
            pltpu.SemaphoreType.DMA((APPLIES, 5)),
            pltpu.SemaphoreType.DMA((APPLIES, 5)),
            pltpu.SemaphoreType.DMA((everyone,)),
            pltpu.SemaphoreType.DMA((everyone,)),
            pltpu.SemaphoreType.DMA((DEGREE + 1, n_src)),
            pltpu.SemaphoreType.DMA((DEGREE + 1, n_src)),
        ],
        compiler_params=pltpu.CompilerParams(
            collective_id=0, has_side_effects=True, vmem_limit_bytes=62 * 1024 * 1024
        ),
    )(start_fields, adjoint_fields, conductivity, surface_rows, source_cells)


def solution(mesh):
    fields = P(("parts", "src"), None, "space", "depth", None)
    return jax.shard_map(
        functools.partial(local, mesh.shape["space"], mesh.shape["src"]),
        mesh=mesh,
        in_specs=(
            fields,
            fields,
            P(("parts", "space"), "depth", None),
            P(("parts", "space"), None),
            P(("parts", "src")),
        ),
        out_specs=(fields, P(("parts", "space"), "depth", "src")),
        check_vma=False,
    )
```

```python
import functools

import jax
import jax.numpy as jnp
from jax import lax
from jax.experimental import pallas as pl
from jax.experimental.pallas import tpu as pltpu
from jax.sharding import PartitionSpec as P

ITERS = 3
ALPHA = 2.0
AIR = 0.01
SOURCE_AMP = 10.0
CENTRE = 6.5
HALF = 6.5
DEGREE = 2 * ITERS
APPLIES = DEGREE + 1
PAD = 8
MESH = pl.DeviceIdType.MESH


def times_operator(poly):
    out = [None] * (len(poly) + 1)

    def add(k, term):
        out[k] = term if out[k] is None else out[k] + term

    for k, c in enumerate(poly):
        add(k, CENTRE * c)
        if k == 0:
            add(1, HALF * c)
        else:
            add(k + 1, (0.5 * HALF) * c)
            add(k - 1, (0.5 * HALF) * c)
    return out


def axpy(a, scale, b):
    out = []
    for k in range(max(len(a), len(b))):
        if k >= len(b):
            out.append(a[k])
        elif k >= len(a):
            out.append(scale * b[k])
        else:
            out.append(a[k] + scale * b[k])
    return out


def with_first(poly, moments):
    total = poly[0] * moments[0]
    for k in range(1, len(poly)):
        total = total + poly[k] * moments[k]
    return total


def inner(a, b, moments):
    total = None
    for i, u in enumerate(a):
        row = None
        for j, w in enumerate(b):
            term = w * (0.5 * (moments[i + j] + moments[abs(i - j)]))
            row = term if row is None else row + term
        total = u * row if total is None else total + u * row
    return total


def field_coefficients(moments):
    one = jnp.ones_like(moments[0])
    r = [one]
    p = [one]
    rho = moments[0]
    x = []
    for step in range(ITERS):
        v = times_operator(p)
        alpha = rho / with_first(v, moments)
        s = axpy(r, -alpha, v)
        t = times_operator(s)
        omega = inner(t, s, moments) / inner(t, t, moments)
        x = axpy(axpy(x, alpha, p), omega, s)
        if step + 1 < ITERS:
            r = axpy(s, -omega, t)
            rho_new = with_first(r, moments)
            beta = rho_new / rho * (alpha / omega)
            p = axpy(r, beta, axpy(p, -omega, v))
            rho = rho_new
    return x


def kernel(
    sizes,
    start_ref,
    adj_ref,
    cond_ref,
    surf_ref,
    cell_ref,
    out_ref,
    grad_ref,
    basis,
    right_in,
    left_in,
    left_out,
    rows_out,
    rows_in,
    edge_out,
    edge_in,
    mass,
    adj,
    cond,
    surf,
    cell,
    dots,
    dots_in,
    weights,
    share_out,
    share_in,
    load_sem,
    send_sem,
    recv_sem,
    dot_send,
    dot_recv,
    share_send,
    share_recv,
):
    n_space, n_src, cx, cz, cy = sizes
    group = n_space * 2
    everyone = group * n_src
    share = cy // n_src
    last = cx - 1
    s = lax.axis_index("space")
    d = lax.axis_index("depth")
    c = lax.axis_index("src")
    me = c * group + s * 2 + d

    def member(g):
        return {"src": g // group, "space": lax.rem(g, group) // 2, "depth": lax.rem(g, 2)}

    def other(k):
        return lax.rem(me + k, everyone)

    def source(k):
        return {"src": lax.rem(c + k, n_src)}

    own = pl.ds(PAD, cz)
    load = pltpu.make_async_copy(start_ref.at[0], basis.at[0, :, :, own, :], load_sem.at[0])
    load.start()
    barrier = pltpu.get_barrier_semaphore()

    def greet(k, carry):
        pl.semaphore_signal(barrier, inc=1, device_id=member(other(k)), device_id_type=MESH)
        return carry

    near_only = 2 <= n_space < DEGREE
    if near_only:
        for target in [{"depth": 1 - d}] + [source(k) for k in range(1, n_src)]:
            pl.semaphore_signal(barrier, inc=1, device_id=target, device_id_type=MESH)
        for present, side in ((s > 0, s - 1), (s < n_space - 1, s + 1)):

            @pl.when(present)
            def _():
                for half in (d, 1 - d):
                    pl.semaphore_signal(
                        barrier,
                        inc=1,
                        device_id={"space": side, "depth": half},
                        device_id_type=MESH,
                    )

    else:
        lax.fori_loop(1, everyone, greet, 0)
    load_cond = pltpu.make_async_copy(cond_ref, cond, load_sem.at[1])
    load_surf = pltpu.make_async_copy(surf_ref, surf, load_sem.at[2])
    load_cell = pltpu.make_async_copy(cell_ref, cell, load_sem.at[3])
    load_adj = pltpu.make_async_copy(adj_ref.at[0], adj, load_sem.at[4])
    load_surf.start()
    load_cond.start()
    load_cell.start()
    load_adj.start()

    lane = lax.broadcasted_iota(jnp.int32, (cz, cy), 1)
    row = lax.broadcasted_iota(jnp.int32, (cz, cy), 0)
    first_lane = lane == 0
    last_lane = lane == cy - 1
    z_start = d * cz
    zero_row = jnp.zeros((1, cy), jnp.float32)

    def earth(x):
        return (z_start + row) >= surf[pl.ds(x, 1), :]

    zero_rows = jnp.zeros((3, cx, 1, cy), jnp.float32)

    def clear(j, carry):
        basis[j, :, :, PAD - 1 : PAD, :] = zero_rows
        basis[j, :, :, PAD + cz : PAD + cz + 1, :] = zero_rows
        right_in[j, 1, PAD - 1 : PAD, :] = zero_row
        rows_out[j] = jnp.zeros((16, cy), jnp.float32)
        return carry

    lax.fori_loop(0, APPLIES, clear, 0)

    @pl.when(s == 0)
    def _():
        left_in[...] = jnp.zeros(left_in.shape, jnp.float32)

    @pl.when(s == n_space - 1)
    def _():
        def blank(j, carry):
            right_in[j, :, own, :] = jnp.zeros((2, cz, cy), jnp.float32)
            return carry

        lax.fori_loop(0, APPLIES, blank, 0)

    def before(f):
        return jnp.where(first_lane, 0.0, pltpu.roll(f, 1, 1))

    def after(f):
        return jnp.where(last_lane, 0.0, pltpu.roll(f, cy - 1, 1))

    def copy(j, kind):
        if kind == 0:
            src, dst, where = left_out.at[j], left_in.at[j], {"space": s + 1}
        elif kind == 1:
            src = basis.at[j, pl.ds(1, 2), 0, own, :]
            dst, where = right_in.at[j, :, own, :], {"space": s - 1}
        else:
            where = {"depth": 1 - d}
            if kind == 2:
                src, dst = rows_out.at[j], rows_in.at[j]
            else:
                src, dst = edge_out.at[j, kind - 3], edge_in.at[j, kind - 3]
                where["space"] = s + 1 if kind == 3 else s - 1
        return pltpu.make_async_remote_copy(
            src_ref=src,
            dst_ref=dst,
            send_sem=send_sem.at[j, kind],
            recv_sem=recv_sem.at[j, kind],
            device_id=where,
            device_id_type=MESH,
        )

    has_left = s > 0
    has_right = s < n_space - 1

    edge = PAD + (cz - 1) * (1 - d)

    def send_right(j):
        edge_out[j, 0] = jnp.broadcast_to(basis[j, 0, last, pl.ds(edge, 1), :], (8, cy))

        @pl.when(has_right)
        def _():
            copy(j, 3).start()

        e0 = basis[j, 0, last, own, :]
        left_out[j, 0] = basis[j, 1, last, own, :] + after(e0) - e0
        left_out[j, 1] = basis[j, 2, last, own, :] + basis[j, 0, last, pl.ds(PAD + 1, cz), :] - e0

        @pl.when(has_right)
        def _():
            copy(j, 0).start()

    def send_left(j):
        edge_out[j, 1] = jnp.broadcast_to(basis[j, 2, 0, pl.ds(edge, 1), :], (8, cy))

        @pl.when(has_left)
        def _():
            copy(j, 4).start()
            copy(j, 1).start()

    def send_rows(j):
        for q in range(3):
            for x in range(cx):
                rows_out[j, q * cx + x : q * cx + x + 1, :] = basis[j, q, x, pl.ds(edge, 1), :]
        copy(j, 2).start()

    def take_rows(j):
        copy(j, 2).wait_recv()
        target = PAD - 1 + (cz + 1) * (1 - d)
        for q in range(3):
            for x in range(cx):
                basis[j, q, x, pl.ds(target, 1), :] = rows_in[j, q * cx + x : q * cx + x + 1, :]

    def take_left(j):
        @pl.when(has_left)
        def _():
            copy(j, 3).wait_recv()
            copy(j, 0).wait_recv()

            @pl.when(d == 0)
            def _():
                left_in[j, 1, cz - 1 : cz, :] = (
                    left_in[j, 1, cz - 1 : cz, :] + edge_in[j, 0, 0:1, :]
                )

    def take_right(j):
        @pl.when(has_right)
        def _():
            copy(j, 4).wait_recv()
            copy(j, 1).wait_recv()

            @pl.when(d == 1)
            def _():
                right_in[j, 1, PAD - 1 : PAD, :] = edge_in[j, 1, 0:1, :]

    below = pl.ds(PAD - 1, cz)
    above = pl.ds(PAD + 1, cz)

    def plane(j, x, shift):
        e0 = basis[j, 0, x, own, :]
        e1 = basis[j, 1, x, own, :]
        e2 = basis[j, 2, x, own, :]
        e0a = basis[j, 0, x, above, :]
        e1a = basis[j, 1, x, above, :]
        b1 = e1 - before(e1)
        b2 = e2 - basis[j, 2, x, below, :]
        if x == last:
            e1p = right_in[j, 0, own, :]
            e2p = right_in[j, 1, own, :]
            e2pb = right_in[j, 1, below, :]
        else:
            e1p = basis[j, 1, x + 1, own, :]
            e2p = basis[j, 2, x + 1, own, :]
            e2pb = basis[j, 2, x + 1, below, :]
        if x == 0:
            l1 = left_in[j, 0]
            l2 = left_in[j, 1]
        else:
            e0m = basis[j, 0, x - 1, own, :]
            l1 = basis[j, 1, x - 1, own, :] + (after(e0m) - e0m)
            l2 = basis[j, 2, x - 1, own, :] + (basis[j, 0, x - 1, above, :] - e0m)
        m = mass[x] + (4.0 - shift)
        g = (e1p - before(e1p)) + (e2p - e2pb) - (b1 + b2)
        q = b2 + e0
        o0 = m * e0 - (after(e0) + before(e0)) - (e0a + basis[j, 0, x, below, :]) + g
        o1 = m * e1 - (e1a + basis[j, 1, x, below, :]) - (e1p + l1) + (after(q) - q)
        o2 = (
            m * e2
            - (after(e2) + before(e2))
            - (e2p + l2)
            + ((e1a - before(e1a) + e0a) - (b1 + e0))
        )
        return o0, o1, o2

    def fold(f):
        return jnp.sum(f.reshape(cz // 8, 8, cy), axis=0)

    def finish(j, x, mode, sums):
        shift = 0.0 if mode == 0 else CENTRE
        outs = plane(j, x, shift)
        same, cross = sums
        for q in range(3):
            if mode == 0:
                new = -outs[q]
                if q == 0:
                    flat = ((s * cx + x) * (2 * cz) + z_start + row) * cy + lane
                    new = new + jnp.where(flat == cell[0], SOURCE_AMP, 0.0)
            else:
                old = basis[j, q, x, own, :]
                if mode == 1:
                    new = (1.0 / HALF) * outs[q]
                else:
                    new = (2.0 / HALF) * outs[q] - basis[j - 1, q, x, own, :]
                cross = cross + fold(new * old)
            basis[j + 1, q, x, own, :] = new
            same = same + fold(new * new)
        return same, cross

    zero_sum = jnp.zeros((8, cy), jnp.float32)

    def packed(planes, target):
        out = []
        for a in range(cx // n_src):
            whole = None
            for b in range(n_src):
                moved = pltpu.roll(
                    planes[a * n_src + b], lax.rem((b - target + n_src) * share, cy), 1
                )
                keep = (lane >= b * share) & (lane < (b + 1) * share)
                whole = moved if b == 0 else jnp.where(keep, moved, whole)
            out.append(whole)
        return out

    def share_copy(e, k):
        return pltpu.make_async_remote_copy(
            src_ref=share_out.at[e, k],
            dst_ref=share_in.at[e, k],
            send_sem=share_send.at[e, k],
            recv_sem=share_recv.at[e, k],
            device_id=source(k),
            device_id_type=MESH,
        )

    def send_shares(e):
        planes = []
        for x in range(cx):
            amount = basis[e, 0, x, own, :] * adj[0, x]
            for q in range(1, 3):
                amount = amount + basis[e, q, x, own, :] * adj[q, x]
            planes.append(amount)
        for k in range(n_src):
            for a, value in enumerate(packed(planes, lax.rem(c + k, n_src))):
                share_out[e, k, a] = value
            if k:
                share_copy(e, k).start()

    def step(j, mode, final, right_first):
        sums = (zero_sum, zero_sum)
        take_rows(j)
        for x in range(1, last):
            sums = finish(j, x, mode, sums)
        for right in (right_first, not right_first):
            if right:
                take_right(j)
                sums = finish(j, last, mode, sums)
                if not final:
                    send_right(j + 1)
            else:
                take_left(j)
                sums = finish(j, 0, mode, sums)
                if not final:
                    send_left(j + 1)
        if not final:
            send_rows(j + 1)
            send_shares(j + 1)
        if mode == 0:
            dots[0] = sums[0]
        else:
            dots[2 * j - 1] = sums[1]
            dots[2 * j] = sums[0]

    load.wait()
    if near_only:
        inside = has_left & has_right

        @pl.when(inside)
        def _():
            pl.semaphore_wait(barrier, n_src + 4)

        @pl.when(jnp.logical_not(inside))
        def _():
            pl.semaphore_wait(barrier, n_src + 2)

    else:
        pl.semaphore_wait(barrier, everyone - 1)
    send_right(0)
    send_left(0)
    send_rows(0)
    load_surf.wait()
    load_cond.wait()
    load_cell.wait()
    for x in range(cx):
        mass[x] = ALPHA * jnp.where(earth(x), cond[x], AIR)
    load_adj.wait()
    send_shares(0)
    step(0, 0, False, False)
    step(1, 1, False, True)

    def middle(i, carry):
        step(2 * i, 2, False, False)
        step(2 * i + 1, 2, False, True)
        return carry

    lax.fori_loop(1, ITERS, middle, 0)
    step(DEGREE, 2, True, False)

    count = 2 * DEGREE + 1
    for k in range(count, 16):
        dots[k] = zero_sum
    mine = jnp.sum(jnp.sum(dots[...], axis=1), axis=1, keepdims=True)
    diagonal = lax.broadcasted_iota(jnp.int32, (16, cy), 0) == lax.broadcasted_iota(
        jnp.int32, (16, cy), 1
    )
    dots_in[me] = jnp.sum(jnp.where(diagonal, mine, 0.0), axis=0, keepdims=True)

    def dot_copy(slot, k):
        return pltpu.make_async_remote_copy(
            src_ref=dots_in.at[slot],
            dst_ref=dots_in.at[slot],
            send_sem=dot_send.at[k],
            recv_sem=dot_recv.at[slot],
            device_id=member(other(k)),
            device_id_type=MESH,
        )

    def dot_start(k, carry):
        dot_copy(me, k).start()
        return carry

    def dot_take(k, carry):
        dot_copy(other(k), k).wait_recv()
        return carry

    for e in range(DEGREE + 1):
        for k in range(1, n_src):
            share_copy(e, k).wait_recv()
    lax.fori_loop(1, everyone, dot_start, 0)
    lax.fori_loop(1, everyone, dot_take, 0)
    table = None
    source_row = lax.broadcasted_iota(jnp.int32, (8, cy), 0)
    for q in range(n_src):
        total = dots_in[q * group]
        for g in range(1, group):
            total = total + dots_in[q * group + g]
        total = jnp.broadcast_to(total, (8, cy))
        table = total if q == 0 else jnp.where(source_row == q, total, table)
    moments = []
    for k in range(count):
        value = jnp.broadcast_to(table[:, k : k + 1], (8, cy))
        moments.append(value if k < 2 else 2.0 * value - moments[k % 2])
    for k, value in enumerate(field_coefficients(moments)):
        weights[k] = value

    coefficients = [weights[k, pl.ds(c, 1), :] for k in range(DEGREE)]
    for x in range(cx):
        for q in range(3):
            value = basis[0, q, x, own, :]
            for k, weight in enumerate(coefficients):
                value = value + weight * basis[k + 1, q, x, own, :]
            out_ref[0, q, x] = value
    summed = []
    for a in range(cx // n_src):
        value = None
        for k in range(n_src):
            origin = lax.rem(c + n_src - k, n_src)
            held = share_in if k else share_out
            term = held[0, k, a]
            value = term if value is None else value + term
            for e in range(DEGREE):
                value = value + weights[e, pl.ds(origin, 1), :] * held[e + 1, k, a]
        summed.append(value)
    for x in range(cx):
        a, b = divmod(x, n_src)
        scale = jnp.where(earth(x), -mass[x], 0.0)
        scale = pltpu.roll(scale, lax.rem((n_src - c) * share, cy), 1)
        value = summed[a] if b == 0 else pltpu.roll(summed[a], cy - b * share, 1)
        grad_ref[x] = (scale * value)[:, :share]

    def dot_drain(k, carry):
        dot_copy(me, k).wait_send()
        return carry

    lax.fori_loop(1, everyone, dot_drain, 0)
    for e in range(DEGREE + 1):
        for k in range(1, n_src):
            share_copy(e, k).wait_send()

    def drain(j, carry):
        copy(j, 2).wait_send()

        @pl.when(has_right)
        def _():
            copy(j, 0).wait_send()
            copy(j, 3).wait_send()

        @pl.when(has_left)
        def _():
            copy(j, 1).wait_send()
            copy(j, 4).wait_send()

        return carry

    lax.fori_loop(0, APPLIES, drain, 0)


def local(n_space, n_src, start_fields, adjoint_fields, conductivity, surface_rows, source_cells):
    _, _, cx, cz, cy = start_fields.shape
    everyone = n_space * 2 * n_src
    f32 = jnp.float32
    vmem = pl.BlockSpec(memory_space=pltpu.VMEM)
    shares = (DEGREE + 1, n_src, cx // n_src, cz, cy)
    return pl.pallas_call(
        functools.partial(kernel, (n_space, n_src, cx, cz, cy)),
        out_shape=(
            jax.ShapeDtypeStruct(start_fields.shape, f32),
            jax.ShapeDtypeStruct((cx, cz, cy // n_src), f32),
        ),
        in_specs=[pl.BlockSpec(memory_space=pltpu.HBM)] * 5,
        out_specs=(vmem, vmem),
        scratch_shapes=[
            pltpu.VMEM((APPLIES + 1, 3, cx, cz + 2 * PAD, cy), f32),
            pltpu.VMEM((APPLIES, 2, cz + 2 * PAD, cy), f32),
            pltpu.VMEM((APPLIES, 2, cz, cy), f32),
            pltpu.VMEM((APPLIES, 2, cz, cy), f32),
            pltpu.VMEM((APPLIES, 16, cy), f32),
            pltpu.VMEM((APPLIES, 16, cy), f32),
            pltpu.VMEM((APPLIES, 2, 8, cy), f32),
            pltpu.VMEM((APPLIES, 2, 8, cy), f32),
            pltpu.VMEM((cx, cz, cy), f32),
            pltpu.VMEM((3, cx, cz, cy), f32),
            pltpu.VMEM((cx, cz, cy), f32),
            pltpu.VMEM((cx, cy), jnp.int32),
            pltpu.SMEM((1,), jnp.int32),
            pltpu.VMEM((16, 8, cy), f32),
            pltpu.VMEM((everyone, 1, cy), f32),
            pltpu.VMEM((DEGREE, 8, cy), f32),
            pltpu.VMEM(shares, f32),
            pltpu.VMEM(shares, f32),
            pltpu.SemaphoreType.DMA((5,)),
            pltpu.SemaphoreType.DMA((APPLIES, 5)),
            pltpu.SemaphoreType.DMA((APPLIES, 5)),
            pltpu.SemaphoreType.DMA((everyone,)),
            pltpu.SemaphoreType.DMA((everyone,)),
            pltpu.SemaphoreType.DMA((DEGREE + 1, n_src)),
            pltpu.SemaphoreType.DMA((DEGREE + 1, n_src)),
        ],
        compiler_params=pltpu.CompilerParams(
            collective_id=0, has_side_effects=True, vmem_limit_bytes=62 * 1024 * 1024
        ),
    )(start_fields, adjoint_fields, conductivity, surface_rows, source_cells)


def solution(mesh):
    fields = P(("parts", "src"), None, "space", "depth", None)
    return jax.shard_map(
        functools.partial(local, mesh.shape["space"], mesh.shape["src"]),
        mesh=mesh,
        in_specs=(
            fields,
            fields,
            P(("parts", "space"), "depth", None),
            P(("parts", "space"), None),
            P(("parts", "src")),
        ),
        out_specs=(fields, P(("parts", "space"), "depth", "src")),
        check_vma=False,
    )
```
